512 devices in a mesh: rows: 128 (over y, z, core), cols: 4 (over x).
Axes of the slice: x: 4, y: 4, z: 16, core: 2. Of those that a mesh axis runs over, the one named last changes fastest.
Arguments:
- factor: float32 [53248, 1664], P('rows', 'cols'), may hold values from -1 to 2, as said below
- slab: float32 [53248, 2048], P('rows', 'cols'), may hold values from -6 to 6
Outputs:
- result: float32 [53248, 2048], P('rows', 'cols')
The draws below stay inside these ranges and needn't reach their ends.
Inputs may be any that keep to these rules, and one draw needn't show every extreme that they name: factor is zero above the diagonal in its first 1664 rows; its diagonal entries lie between 1 and 2.
All inputs are finite; a program needn't handle non-finite values.
Results may differ from the reference program's by a relative error of at most 0.0001.
Values sent between devices are 32-bit elements; how exact they have to be, the bound alone decides.
A program may use at most 64 MiB of HBM per device.

```python
import jax
import jax.numpy as jnp
from jax import lax

PB = 416
PANELS = 4
SLAB = 2048
K = 1664
N_ORDER = 53248


def draw_factor(key, part):
    key_off = jax.random.fold_in(key, 11)
    key_low = jax.random.fold_in(key, 12)
    key_diag = jax.random.fold_in(key, 13)
    shape = (N_ORDER, K)
    off_vals = jnp.clip(jax.random.normal(key_off, shape, jnp.float32), -4.0, 4.0) / jnp.sqrt(jnp.float32(K))
    low_vals = 0.6 * jnp.clip(jax.random.normal(key_low, shape, jnp.float32), -4.0, 4.0) / jnp.sqrt(jnp.float32(PB))
    diag_vals = jax.random.uniform(key_diag, shape, jnp.float32, 1.0, 2.0)
    row_ids = lax.broadcasted_iota(jnp.int32, shape, 0)
    col_ids = lax.broadcasted_iota(jnp.int32, shape, 1)
    row_block = row_ids // PB
    col_block = col_ids // PB
    row_in = row_ids % PB
    col_in = col_ids % PB
    inside = jnp.where(row_in > col_in, low_vals, jnp.where(row_in == col_in, diag_vals, 0.0))
    return jnp.where(row_block == col_block, inside, jnp.where(row_block > col_block, off_vals, 0.0)).astype(jnp.float32)


def shard_levels(key, dims, split, low, largest):
    factor_of = 1.0
    for axis_at, parts in split:
        steps = jax.random.uniform(jax.random.fold_in(jax.random.fold_in(key, 6), axis_at), (parts,), jnp.float32, low / len(split), largest / len(split))
        factor_of = factor_of * jnp.repeat(jnp.exp(steps), dims[axis_at] // parts).reshape((-1,) + (1,) * (len(dims) - 1 - axis_at))
    return factor_of


def normal_values(key, shape, spread, bound, split=(), held_as=jnp.bfloat16):
    loudness = shard_levels(key, shape, split, -0.22, 0.18) if split else 1.0
    values = jax.random.normal(key, shape, jnp.float32) * spread * loudness
    return jnp.minimum(jnp.maximum(values, -bound), bound).astype(held_as)


def setup_inputs(seed: int = 0) -> dict:
    arg_keys = jax.random.split(jax.random.key(seed), 3)
    return {
        "factor": draw_factor(jax.random.fold_in(arg_keys[2], 71), 0),
        "slab": normal_values(arg_keys[1], (N_ORDER, SLAB), 1.0, 6.0, ((0, 128), (1, 4)), jnp.float32),
    }


def reference(factor, slab):
    current = slab
    for panel in range(PANELS):
        offset = panel * PB
        panel_cols = factor[:, offset:offset + PB]
        solved = lax.linalg.triangular_solve(panel_cols[offset:offset + PB], current[offset:offset + PB], left_side=True, lower=True)
        current = current - jnp.dot(panel_cols, solved, precision=lax.Precision.HIGHEST)
        current = current.at[offset:offset + PB].set(solved)
    return current
```

```python
import functools

import jax
import jax.numpy as jnp
from jax import lax
from jax.experimental import pallas as pl
from jax.experimental.pallas import tpu as pltpu
from jax.sharding import PartitionSpec as P

MESH = pl.DeviceIdType.MESH
HI = lax.Precision.HIGHEST

PB = 416
PANELS = 4
SLABC = 512
HALF = PB // 2
ST = 128
NY, NZ, NC = 4, 16, 2
BLOCKS = ((0, 128), (128, 128), (256, 128), (384, 32))


def split(value):
    high = value.astype(jnp.bfloat16)
    low = (value - high.astype(jnp.float32)).astype(jnp.bfloat16)
    return high, low


def dot3(left, right):
    dot = functools.partial(jnp.dot, preferred_element_type=jnp.float32)
    return dot(left[0], right[0]) + (dot(left[0], right[1]) + dot(left[1], right[0]))


def invert_blocks(tri, inv):
    mats, outs = [], []
    for r0, n in BLOCKS:
        t = tri[r0 : r0 + n, r0 : r0 + n]
        row = lax.broadcasted_iota(jnp.int32, (n, n), 0)
        col = lax.broadcasted_iota(jnp.int32, (n, n), 1)
        mats.append((t, row, col))
        outs.append(jnp.where(row == col, 1.0 / jnp.where(row == col, t, 1.0), 0.0))
    m = 1
    while m < 128:
        for j, (r0, n) in enumerate(BLOCKS):
            if m >= n:
                continue
            t, row, col = mats[j]
            below = (row // (2 * m) == col // (2 * m)) & (row % (2 * m) >= m) & (col % (2 * m) < m)
            c = jnp.where(below, t, 0.0)
            o = outs[j]
            cm = jnp.dot(c, o, precision=HI)
            outs[j] = o - jnp.dot(o, cm, precision=HI)
        m *= 2
    for j, (r0, n) in enumerate(BLOCKS):
        inv[j, 0:n, 0:n] = outs[j]


def kernel(f_ref, b_ref, out, lbuf, inv, xbuf, lsend, lrecv, isend, irecv, zsend, zrecv, ysend, yrecv, csend, crecv, ssend):
    r = lax.axis_index("rows")
    c = lax.axis_index("cols")
    y = r // (NZ * NC)
    z = (r // NC) % NZ
    k = r % NC

    def dev(y_, z_, k_):
        return (y_ * (NZ * NC) + z_ * NC + k_, c)

    def at_x(step):
        return (r, (c + step) % PANELS)

    def at_y(step):
        return dev((y + step) % NY, z, k)

    def at_z(step):
        return dev(y, (z + step + NZ) % NZ, k)

    sibling = dev(y, z, 1 - k)

    barrier = pltpu.get_barrier_semaphore()
    partners = [at_x(1), at_x(2), at_x(3), at_y(1), at_y(2), at_y(3)]
    partners += [at_z(s) for s in (1, -1, 3, -3, 5, -5)] + [sibling]
    for partner in partners:
        pl.semaphore_signal(barrier, inc=1, device_id=partner, device_id_type=MESH)
    pl.semaphore_wait(barrier, len(partners))

    def copy(src, dst, send, recv, to):
        return pltpu.make_async_remote_copy(
            src_ref=src, dst_ref=dst, send_sem=send, recv_sem=recv, device_id=to, device_id_type=MESH
        )

    def half(ref, h):
        return ref.at[pl.ds(h * HALF, HALF), :]

    def lhalf(p, h):
        return lbuf.at[p, pl.ds(h * HALF, HALF), :]

    def own_factor():
        for i, (step, h) in enumerate(((1, 0), (3, 1), (1, 1), (3, 0))):
            yield copy(half(f_ref, h), lhalf(c, h), lsend.at[i], lrecv.at[c, h], at_x(step))

    def pass_on(step, h):
        p = (c + 4 - step) % PANELS
        return p, copy(lhalf(p, h), lhalf(p, h), lsend.at[4 + h], lrecv.at[p, h], at_x(step))

    def factor_arrived(p, h):
        copy(lhalf(p, h), lhalf(p, h), lsend.at[0], lrecv.at[p, h], sibling).wait_recv()

    def inverses():
        for i in range(3):
            yield copy(inv, inv, isend.at[i], irecv.at[0], at_x(i + 1))

    @pl.when(r >= c)
    def _():
        for cp in own_factor():
            cp.start()

    @pl.when(r == c)
    def _():
        inv[...] = jnp.zeros_like(inv)
        invert_blocks(f_ref, inv)
        for cp in inverses():
            cp.start()

    lbuf[c] = f_ref[...]
    out[...] = b_ref[...]

    for step, h in ((1, 0), (3, 1)):
        p, onward = pass_on(step, h)

        @pl.when(r >= p)
        def _():
            factor_arrived(p, h)
            onward.start()

    def rest_of_factor(p):
        @pl.when(p == (c + 1) % PANELS)
        def _():
            factor_arrived(p, 0)

        @pl.when(p == (c + 3) % PANELS)
        def _():
            factor_arrived(p, 1)

        @pl.when(p == (c + 2) % PANELS)
        def _():
            factor_arrived(p, 0)
            factor_arrived(p, 1)

    def piece(p, h, s):
        return xbuf.at[p, s, pl.ds(h * HALF, HALF), :]

    def for_z(p, do):
        d = (z - p // 2 + NZ) % NZ
        mine = piece(p, k, y)
        steps = (
            (5, (d == 0)),
            (-5, (d == 0)),
            (1, (d == 0) | (d == 1) | (d == 2) | (d == 3) | (d == 5) | (d == 6)),
            (-1, (d == 0) | (d == 15) | (d == 14) | (d == 13) | (d == 11) | (d == 10)),
            (3, (d == 5)),
        )
        for i, (step, cond) in enumerate(steps):

            @pl.when(cond)
            def _():
                do(copy(mine, mine, zsend.at[p, i], zrecv.at[p], at_z(step)))

    def for_y(p, do):
        d = (z - p // 2 + NZ) % NZ
        mine = piece(p, k, y)
        for i in range(3):
            to = (y + i + 1) % NY

            @pl.when((to != 0) | (d != 0))
            def _():
                do(copy(mine, mine, ysend.at[p, i], yrecv.at[p, y], dev(to, z, k)))

    def for_scatter(p, do):
        for s in range(1, NY):
            it = piece(p, k, s)
            do(copy(it, it, ssend.at[p, s], zrecv.at[p], dev(s, z, k)))

    def to_sibling(p, h, s):
        it = piece(p, h, s)
        return copy(it, it, csend.at[p, h, s], crecv.at[p, h, s], sibling)

    def start(cp):
        cp.start()

    def wait_send(cp):
        cp.wait_send()

    def roles(p):
        chip = (y == 0) & (z == p // 2)
        source = r == p
        return source, chip & (r != p), jnp.logical_not(chip)

    def as_root(p, do):
        for_scatter(p, do)
        for_z(p, do)
        for_y(p, do)

    def panel(p, carry):
        source, helper, other = roles(p)

        @pl.when(source)
        def _():
            rest_of_factor(p)

            @pl.when(c != p)
            def _():
                copy(inv, inv, isend.at[0], irecv.at[0], sibling).wait_recv()

            for j, (r0, n) in enumerate(BLOCKS):
                solved = jnp.dot(inv[j, 0:n, 0:n], out[r0 : r0 + n, :], precision=HI)
                out[r0 : r0 + n, :] = solved
                for s in range(NY):
                    xbuf[p, s, r0 : r0 + n, :] = solved[:, s * ST : (s + 1) * ST]
                if r0 + n < PB:
                    below = lbuf[p, r0 + n : PB, r0 : r0 + n]
                    out[r0 + n : PB, :] -= jnp.dot(below, solved, precision=HI)
                if j in (1, 3):
                    h = j // 2
                    for s in range(NY):
                        to_sibling(p, h, s).start()

                    @pl.when(k == h)
                    def _():
                        as_root(p, start)

        @pl.when(helper)
        def _():
            for s in range(NY):
                to_sibling(p, k, s).wait_recv()
            as_root(p, start)
            for s in range(NY):
                to_sibling(p, 1 - k, s).wait_recv()

        @pl.when(other)
        def _():
            mine = piece(p, k, y)
            copy(mine, mine, zsend.at[p, 0], zrecv.at[p], sibling).wait_recv()
            for_z(p, start)
            for_y(p, start)
            to_sibling(p, k, y).start()
            for i in range(1, NY):
                s = (y + i) % NY
                it = piece(p, k, s)
                copy(it, it, ysend.at[p, 0], yrecv.at[p, s], sibling).wait_recv()
                to_sibling(p, k, s).start()
            for s in range(NY):
                to_sibling(p, 1 - k, s).wait_recv()

        @pl.when(r > p)
        def _():
            rest_of_factor(p)
            x = jnp.concatenate([xbuf[p, s] for s in range(NY)], axis=1)
            out[...] -= dot3(split(lbuf[p]), split(x))

        return carry

    lax.fori_loop(0, PANELS, panel, 0)

    def drain(p, carry):
        source, helper, other = roles(p)

        @pl.when(source)
        def _():
            for h in range(2):
                for s in range(NY):
                    to_sibling(p, h, s).wait_send()

        @pl.when(source | helper)
        def _():
            for_scatter(p, wait_send)

        for_z(p, wait_send)
        for_y(p, wait_send)

        @pl.when(other)
        def _():
            for s in range(NY):
                to_sibling(p, k, s).wait_send()

        return carry

    lax.fori_loop(0, PANELS, drain, 0)

    @pl.when(r >= c)
    def _():
        for cp in own_factor():
            cp.wait_send()

    for step, h in ((1, 0), (3, 1)):
        p, onward = pass_on(step, h)

        @pl.when(r >= p)
        def _():
            onward.wait_send()

    @pl.when(r == c)
    def _():
        for cp in inverses():
            cp.wait_send()


def body(factor, slab):
    dma = pltpu.SemaphoreType.DMA
    return pl.pallas_call(
        kernel,
        out_shape=jax.ShapeDtypeStruct((PB, SLABC), jnp.float32),
        in_specs=[pl.BlockSpec(memory_space=pltpu.VMEM)] * 2,
        out_specs=pl.BlockSpec(memory_space=pltpu.VMEM),
        scratch_shapes=[
            pltpu.VMEM((PANELS, PB, PB), jnp.float32),
            pltpu.VMEM((4, 128, 128), jnp.float32),
            pltpu.VMEM((PANELS, NY, PB, ST), jnp.float32),
            dma((6,)),
            dma((PANELS, 2)),
            dma((3,)),
            dma((1,)),
            dma((PANELS, 5)),
            dma((PANELS,)),
            dma((PANELS, 3)),
            dma((PANELS, NY)),
            dma((PANELS, 2, NY)),
            dma((PANELS, 2, NY)),
            dma((PANELS, NY)),
        ],
        compiler_params=pltpu.CompilerParams(
            collective_id=0, has_side_effects=True, vmem_limit_bytes=40 * 1024 * 1024
        ),
        cost_estimate=pl.CostEstimate(flops=2 * 3 * PB * 1664 * SLABC, bytes_accessed=2_500_000, transcendentals=0),
    )(factor, slab)


def solution(mesh):
    return jax.shard_map(
        body,
        mesh=mesh,
        in_specs=(P("rows", "cols"), P("rows", "cols")),
        out_specs=P("rows", "cols"),
        check_vma=False,
    )
```

```python
import functools

import jax
import jax.numpy as jnp
from jax import lax
from jax.experimental import pallas as pl
from jax.experimental.pallas import tpu as pltpu
from jax.sharding import PartitionSpec as P

MESH = pl.DeviceIdType.MESH
HI = lax.Precision.HIGHEST

PB = 416
PANELS = 4
SLABC = 512
HALF = PB // 2
QR = PB // 4
ST = 128
NY, NZ, NC = 4, 16, 2
BLOCKS = ((0, 128), (128, 128), (256, 128), (384, 32))
INV = (0, 416, 704, 864)
BELOW = (128, 544, 832)
PACK = 896
WAYS = ((1, 0), (3, 1), (1, 1), (3, 0))
PARTS = ((0, 416), (416, 480))


def split(value):
    high = value.astype(jnp.bfloat16)
    low = (value - high.astype(jnp.float32)).astype(jnp.bfloat16)
    return high, low


def dot3(left, right):
    dot = functools.partial(jnp.dot, preferred_element_type=jnp.float32)
    return dot(left[0], right[0]) + (dot(left[0], right[1]) + dot(left[1], right[0]))


def pack_panel(tri, pack):
    mats, outs = [], []
    for j, (r0, n) in enumerate(BLOCKS):
        if j < 3:
            pack[BELOW[j] : BELOW[j] + PB - r0 - n, :] = tri[r0 + n : PB, r0 : r0 + n]
        t = tri[r0 : r0 + n, r0 : r0 + n]
        row = lax.broadcasted_iota(jnp.int32, (n, n), 0)
        col = lax.broadcasted_iota(jnp.int32, (n, n), 1)
        mats.append((t, row, col))
        outs.append(jnp.where(row == col, 1.0 / jnp.where(row == col, t, 1.0), 0.0))
    m = 1
    while m < 128:
        for j, (r0, n) in enumerate(BLOCKS):
            if m >= n:
                continue
            t, row, col = mats[j]
            below = (row // (2 * m) == col // (2 * m)) & (row % (2 * m) >= m) & (col % (2 * m) < m)
            c = jnp.where(below, t, 0.0)
            o = outs[j]
            if m == 1:
                by_row = jnp.sum(o, axis=1, keepdims=True)
                by_col = jnp.sum(o, axis=0, keepdims=True)
                outs[j] = o - by_row * c * by_col
            else:
                outs[j] = o - jnp.dot(o, jnp.dot(c, o, precision=HI), precision=HI)
        m *= 2
    pack[INV[3] : PACK, :] = jnp.zeros((32, 128), jnp.float32)
    for j, (r0, n) in enumerate(BLOCKS):
        pack[INV[j] : INV[j] + n, 0:n] = outs[j]


def kernel(
    f_ref, b_ref, out, lbuf, high, low, pack, xbuf, load, lsend, lrecv, isend, irecv, zsend, zrecv, ysend, yrecv, csend, crecv, ssend, dsend, gate
):
    r = lax.axis_index("rows")
    c = lax.axis_index("cols")
    y = r // (NZ * NC)
    z = (r // NC) % NZ
    k = r % NC

    def dev(y_, z_, k_):
        return (y_ * (NZ * NC) + z_ * NC + k_, c)

    def at_x(step):
        return (r, (c + step) % PANELS)

    def at_y(step):
        return dev((y + step) % NY, z, k)

    def at_z(step):
        return dev(y, (z + step + NZ) % NZ, k)

    sibling = dev(y, z, 1 - k)

    barrier = pltpu.get_barrier_semaphore()
    partners = [at_x(1), at_x(2), at_x(3), at_y(1), at_y(2), at_y(3)]
    partners += [at_z(s) for s in (1, -1, 2, -2, 3, -3, 5, -5)] + [sibling]
    for partner in partners:
        pl.semaphore_signal(barrier, inc=1, device_id=partner, device_id_type=MESH)

    load_f = pltpu.make_async_copy(f_ref, lbuf.at[c], load.at[0])
    load_b = pltpu.make_async_copy(b_ref, out, load.at[1])
    load_f.start()
    load_b.start()
    load_f.wait()

    @pl.when(r == c)
    def _():
        pack_panel(lbuf.at[c], pack)

    pl.semaphore_wait(barrier, len(partners))

    def copy(src, dst, send, recv, to):
        return pltpu.make_async_remote_copy(
            src_ref=src, dst_ref=dst, send_sem=send, recv_sem=recv, device_id=to, device_id_type=MESH
        )

    def lhalf(p, h):
        return lbuf.at[p, pl.ds(h * HALF, HALF), :]

    def ppart(h):
        return pack.at[pl.ds(PARTS[h][0], PARTS[h][1]), :]

    def own_pack(i):
        step, h = WAYS[i]
        return copy(ppart(h), ppart(h), isend.at[i], irecv.at[h], at_x(step))

    def pass_pack(step, h):
        return copy(ppart(h), ppart(h), isend.at[4 + h], irecv.at[h], at_x(step))

    def pack_arrived(h):
        copy(ppart(h), ppart(h), isend.at[0], irecv.at[h], sibling).wait_recv()

    def own_factor(i):
        step, h = WAYS[i]
        return copy(lhalf(c, h), lhalf(c, h), lsend.at[i], lrecv.at[c, h], at_x(step))

    def pass_on(step, h):
        p = (c + 4 - step) % PANELS
        return p, copy(lhalf(p, h), lhalf(p, h), lsend.at[4 + h], lrecv.at[p, h], at_x(step))

    def factor_arrived(p, h):
        copy(lhalf(p, h), lhalf(p, h), lsend.at[0], lrecv.at[p, h], sibling).wait_recv()

    def own_sent():
        @pl.when(r == c)
        def _():
            for i in (2, 3):
                own_pack(i).wait_send()

        @pl.when(r > c)
        def _():
            for i in range(4):
                own_factor(i).wait_send()

    first = (r == 0) | (r == 2)

    @pl.when(((r == 1) | (r == 3)) & (r > c))
    def _():
        pl.semaphore_wait(gate, 1)

    @pl.when(r == c)
    def _():
        for i in (0, 1):
            own_pack(i).start()
        for i in (0, 1):
            own_pack(i).wait_send()
        for i in (2, 3):
            own_pack(i).start()

    @pl.when(first & (r == c))
    def _():
        pl.semaphore_signal(gate, inc=1, device_id=sibling, device_id_type=MESH)

    @pl.when(r > c)
    def _():
        own_factor(0).start()
        own_factor(1).start()

    for step, h in ((1, 0), (3, 1)):
        p, onward = pass_on(step, h)

        @pl.when(r == p)
        def _():
            pack_arrived(h)
            pass_pack(step, h).start()

        @pl.when(r > p)
        def _():
            factor_arrived(p, h)
            onward.start()

        @pl.when(r > c)
        def _():
            own_factor(2 + h).start()

    @pl.when(first & (r > c))
    def _():
        own_sent()
        pl.semaphore_signal(gate, inc=1, device_id=sibling, device_id_type=MESH)

    load_b.wait()

    def rest_of_factor(p):
        @pl.when(p == (c + 1) % PANELS)
        def _():
            factor_arrived(p, 0)

        @pl.when(p == (c + 3) % PANELS)
        def _():
            factor_arrived(p, 1)

        @pl.when(p == (c + 2) % PANELS)
        def _():
            factor_arrived(p, 0)
            factor_arrived(p, 1)

    def piece(p, q, s):
        return xbuf.at[p, s, pl.ds(q * QR, QR), :]

    def for_z(p, t, do):
        d = (z - p // 2 + NZ) % NZ
        mine = piece(p, 2 * t + k, y)
        far = d == 0
        near = (p < 2) & (y == 0)
        steps = (
            (4, 1, far & near),
            (0, 5, far & jnp.logical_not(near)),
            (1, -5, far),
            (6, 3, (d == 5) | ((d == 2) & near)),
            (2, 2, (far & jnp.logical_not(near)) | (d == 5)),
            (3, -2, far | (d == 11)),
            (4, 1, ((d == 1) & near) | (d == 2) | (d == 5) | (d == 14) | (d == 11)),
            (5, -1, ((d == 2) & jnp.logical_not(near)) | (d == 5) | (d == 14) | (d == 11)),
        )
        for i, step, cond in steps:

            @pl.when(cond)
            def _():
                do(copy(mine, mine, zsend.at[p, t, i], zrecv.at[p, t], at_z(step)))

    def for_y(p, t, do):
        d = (z - p // 2 + NZ) % NZ
        mine = piece(p, 2 * t + k, y)
        for i in range(3):
            to = (y + i + 1) % NY

            @pl.when(((to != 0) & ((d != 0) | (y != 0) | (to != 2))) | ((to == 0) & (d != 0) & ((p >= 2) | (d != 1))))
            def _():
                do(copy(mine, mine, ysend.at[p, t, i], yrecv.at[p, t, y], dev(to, z, k)))

    def pass_first(p, t, do):
        @pl.when((z == p // 2) & (y == (1 if t == 0 else 3)))
        def _():
            it = piece(p, 2 * t + k, 0)
            do(copy(it, it, ysend.at[p, t, 3], yrecv.at[p, t, 0], dev(2, z, k)))

    def for_scatter(p, t, do):
        for s in (1, 3, 2):
            it = piece(p, 2 * t + k, s)
            do(copy(it, it, ssend.at[p, t, s], zrecv.at[p, t], dev(s, z, k)))

    def for_next(p, t, do):
        @pl.when(p < 2)
        def _():
            for s in range(1, NY):
                it = piece(p, 2 * t + k, s)
                do(copy(it, it, dsend.at[p, t, s], yrecv.at[p, t, s], at_z(1)))

    def to_sibling(p, q, s):
        it = piece(p, q, s)
        return copy(it, it, csend.at[p, q, s], crecv.at[p, q, s], sibling)

    def start(cp):
        cp.start()

    def wait_send(cp):
        cp.wait_send()

    def roles(p):
        chip = (y == 0) & (z == p // 2)
        source = r == p
        return source, chip & (r != p), jnp.logical_not(chip)

    def as_root(p, t, do):
        for_next(p, t, do)
        for_z(p, t, do)
        for_scatter(p, t, do)
        for_y(p, t, do)

    def prepare(p):
        rest_of_factor(p)
        high[...], low[...] = split(lbuf[p])

    def update(p):
        x = jnp.concatenate([xbuf[p, s] for s in range(NY)], axis=1)
        out[...] -= dot3((high[...], low[...]), split(x))

    def panel(p, carry):
        source, helper, other = roles(p)

        @pl.when(source)
        def _():
            @pl.when((p == (c + 1) % PANELS) | (p == (c + 2) % PANELS))
            def _():
                pack_arrived(0)

            @pl.when((p == (c + 3) % PANELS) | (p == (c + 2) % PANELS))
            def _():
                pack_arrived(1)

            for j, (r0, n) in enumerate(BLOCKS):
                solved = jnp.dot(pack[INV[j] : INV[j] + n, 0:n], out[r0 : r0 + n, :], precision=HI)
                out[r0 : r0 + n, :] = solved
                for s in range(NY):
                    xbuf[p, s, r0 : r0 + n, :] = solved[:, s * ST : (s + 1) * ST]
                for s in range(NY):
                    to_sibling(p, j, s).start()

                @pl.when((p % 2 == 1) & (k == j % 2))
                def _():
                    as_root(p, j // 2, start)

                if j < 3:
                    below = pack[BELOW[j] : BELOW[j] + PB - r0 - n, :]
                    out[r0 + n : PB, :] -= jnp.dot(below, solved, precision=HI)

            @pl.when(p % 2 == 0)
            def _():
                for t in range(2):
                    as_root(p, t, start)

        @pl.when(helper)
        def _():
            for t in range(2):
                for s in range(NY):
                    to_sibling(p, 2 * t + k, s).wait_recv()
                as_root(p, t, start)
            for t in range(2):
                for s in range(NY):
                    to_sibling(p, 2 * t + 1 - k, s).wait_recv()

        @pl.when(other)
        def _():
            for t in range(2):
                mine = piece(p, 2 * t + k, y)
                copy(mine, mine, zsend.at[p, t, 0], zrecv.at[p, t], sibling).wait_recv()
                for_z(p, t, start)
                for_y(p, t, start)
                to_sibling(p, 2 * t + k, y).start()

            @pl.when((r > PANELS - 1) & (p > 0))
            def _():
                update(p - 1)

            @pl.when(r > PANELS - 1)
            def _():
                prepare(p)

            for t in range(2):
                for i in (1, 3, 2):
                    s = (y + i) % NY
                    it = piece(p, 2 * t + k, s)
                    copy(it, it, ysend.at[p, t, 0], yrecv.at[p, t, s], sibling).wait_recv()

                    @pl.when(s == 0)
                    def _():
                        pass_first(p, t, start)

                    to_sibling(p, 2 * t + k, s).start()
            for t in range(2):
                for s in range(NY):
                    to_sibling(p, 2 * t + 1 - k, s).wait_recv()

        @pl.when((r > p) & (r < PANELS))
        def _():
            prepare(p)
            update(p)

        return carry

    lax.fori_loop(0, PANELS, panel, 0)

    @pl.when(r > PANELS - 1)
    def _():
        update(PANELS - 1)

    def drain(p, carry):
        source, helper, other = roles(p)

        @pl.when(source)
        def _():
            for q in range(4):
                for s in range(NY):
                    to_sibling(p, q, s).wait_send()

        for t in range(2):

            @pl.when(source | helper)
            def _():
                for_next(p, t, wait_send)
                for_scatter(p, t, wait_send)

            for_z(p, t, wait_send)
            for_y(p, t, wait_send)

            @pl.when(other)
            def _():
                pass_first(p, t, wait_send)
                for s in range(NY):
                    to_sibling(p, 2 * t + k, s).wait_send()

        return carry

    lax.fori_loop(0, PANELS, drain, 0)

    @pl.when(jnp.logical_not(first & (r > c)))
    def _():
        own_sent()

    for step, h in ((1, 0), (3, 1)):
        p, onward = pass_on(step, h)

        @pl.when(r == p)
        def _():
            pass_pack(step, h).wait_send()

        @pl.when(r > p)
        def _():
            onward.wait_send()


def body(factor, slab):
    dma = pltpu.SemaphoreType.DMA
    return pl.pallas_call(
        kernel,
        out_shape=jax.ShapeDtypeStruct((PB, SLABC), jnp.float32),
        in_specs=[pl.BlockSpec(memory_space=pltpu.HBM)] * 2,
        out_specs=pl.BlockSpec(memory_space=pltpu.VMEM),
        scratch_shapes=[
            pltpu.VMEM((PANELS, PB, PB), jnp.float32),
            pltpu.VMEM((PB, PB), jnp.bfloat16),
            pltpu.VMEM((PB, PB), jnp.bfloat16),
            pltpu.VMEM((PACK, 128), jnp.float32),
            pltpu.VMEM((PANELS, NY, PB, ST), jnp.float32),
            dma((2,)),
            dma((6,)),
            dma((PANELS, 2)),
            dma((6,)),
            dma((2,)),
            dma((PANELS, 2, 7)),
            dma((PANELS, 2)),
            dma((PANELS, 2, 4)),
            dma((PANELS, 2, NY)),
            dma((PANELS, 4, NY)),
            dma((PANELS, 4, NY)),
            dma((PANELS, 2, NY)),
            dma((PANELS, 2, NY)),
            pltpu.SemaphoreType.REGULAR,
        ],
        compiler_params=pltpu.CompilerParams(
            collective_id=0, has_side_effects=True, vmem_limit_bytes=40 * 1024 * 1024
        ),
        cost_estimate=pl.CostEstimate(flops=2 * 3 * PB * 1664 * SLABC, bytes_accessed=2_500_000, transcendentals=0),
    )(factor, slab)


def solution(mesh):
    return jax.shard_map(
        body,
        mesh=mesh,
        in_specs=(P("rows", "cols"), P("rows", "cols")),
        out_specs=P("rows", "cols"),
        check_vma=False,
    )
```

```python
import functools

import jax
import jax.numpy as jnp
from jax import lax
from jax.experimental import pallas as pl
from jax.experimental.pallas import tpu as pltpu
from jax.sharding import PartitionSpec as P

MESH = pl.DeviceIdType.MESH
HI = lax.Precision.HIGHEST

PB = 416
PANELS = 4
SLABC = 512
HALF = PB // 2
QR = PB // 4
ST = 128
NY, NZ, NC = 4, 16, 2
BLOCKS = ((0, 128), (128, 128), (256, 128), (384, 32))
INV = (0, 416, 704, 864)
BELOW = (128, 544, 832)
PACK = 896
WAYS = ((1, 0), (3, 1), (1, 1), (3, 0))
PARTS = ((0, 416), (416, 480))


def split(value):
    high = value.astype(jnp.bfloat16)
    low = (value - high.astype(jnp.float32)).astype(jnp.bfloat16)
    return high, low


def dot3(left, right):
    dot = functools.partial(jnp.dot, preferred_element_type=jnp.float32)
    return dot(left[0], right[0]) + (dot(left[0], right[1]) + dot(left[1], right[0]))


def pack_panel(tri, pack):
    mats, outs = [], []
    for j, (r0, n) in enumerate(BLOCKS):
        if j < 3:
            pack[BELOW[j] : BELOW[j] + PB - r0 - n, :] = tri[r0 + n : PB, r0 : r0 + n]
        t = tri[r0 : r0 + n, r0 : r0 + n]
        row = lax.broadcasted_iota(jnp.int32, (n, n), 0)
        col = lax.broadcasted_iota(jnp.int32, (n, n), 1)
        mats.append((t, row, col))
        outs.append(jnp.where(row == col, 1.0 / jnp.where(row == col, t, 1.0), 0.0))
    m = 1
    while m < 128:
        for j, (r0, n) in enumerate(BLOCKS):
            if m >= n:
                continue
            t, row, col = mats[j]
            below = (row // (2 * m) == col // (2 * m)) & (row % (2 * m) >= m) & (col % (2 * m) < m)
            c = jnp.where(below, t, 0.0)
            o = outs[j]
            if m == 1:
                by_row = jnp.sum(o, axis=1, keepdims=True)
                by_col = jnp.sum(o, axis=0, keepdims=True)
                outs[j] = o - by_row * c * by_col
            else:
                outs[j] = o - jnp.dot(o, jnp.dot(c, o, precision=HI), precision=HI)
        m *= 2
    pack[INV[3] : PACK, :] = jnp.zeros((32, 128), jnp.float32)
    for j, (r0, n) in enumerate(BLOCKS):
        pack[INV[j] : INV[j] + n, 0:n] = outs[j]


def kernel(
    f_ref, b_ref, out, lbuf, high, low, pack, xbuf, load, lsend, lrecv, isend, irecv, zsend, zrecv, ysend, yrecv, csend, crecv, ssend, dsend, gate
):
    r = lax.axis_index("rows")
    c = lax.axis_index("cols")
    y = r // (NZ * NC)
    z = (r // NC) % NZ
    k = r % NC

    def dev(y_, z_, k_):
        return (y_ * (NZ * NC) + z_ * NC + k_, c)

    def at_x(step):
        return (r, (c + step) % PANELS)

    def at_y(step):
        return dev((y + step) % NY, z, k)

    def at_z(step):
        return dev(y, (z + step + NZ) % NZ, k)

    sibling = dev(y, z, 1 - k)

    barrier = pltpu.get_barrier_semaphore()
    partners = [at_x(1), at_x(2), at_x(3), at_y(1), at_y(2), at_y(3)]
    partners += [at_z(s) for s in (1, -1, 2, -2, 3, -3, 6, -6)] + [sibling]
    for partner in partners:
        pl.semaphore_signal(barrier, inc=1, device_id=partner, device_id_type=MESH)

    load_f = pltpu.make_async_copy(f_ref, lbuf.at[c], load.at[0])
    load_b = pltpu.make_async_copy(b_ref, out, load.at[1])
    load_f.start()
    load_b.start()
    load_f.wait()

    @pl.when(r == c)
    def _():
        pack_panel(lbuf.at[c], pack)

    pl.semaphore_wait(barrier, len(partners))

    def copy(src, dst, send, recv, to):
        return pltpu.make_async_remote_copy(
            src_ref=src, dst_ref=dst, send_sem=send, recv_sem=recv, device_id=to, device_id_type=MESH
        )

    def lhalf(p, h):
        return lbuf.at[p, pl.ds(h * HALF, HALF), :]

    def ppart(h):
        return pack.at[pl.ds(PARTS[h][0], PARTS[h][1]), :]

    def own_pack(i):
        step, h = WAYS[i]
        return copy(ppart(h), ppart(h), isend.at[i], irecv.at[h], at_x(step))

    def pass_pack(step, h):
        return copy(ppart(h), ppart(h), isend.at[4 + h], irecv.at[h], at_x(step))

    def pack_arrived(h):
        copy(ppart(h), ppart(h), isend.at[0], irecv.at[h], sibling).wait_recv()

    def own_factor(i):
        step, h = WAYS[i]
        return copy(lhalf(c, h), lhalf(c, h), lsend.at[i], lrecv.at[c, h], at_x(step))

    def pass_on(step, h):
        p = (c + 4 - step) % PANELS
        return p, copy(lhalf(p, h), lhalf(p, h), lsend.at[4 + h], lrecv.at[p, h], at_x(step))

    def factor_arrived(p, h):
        copy(lhalf(p, h), lhalf(p, h), lsend.at[0], lrecv.at[p, h], sibling).wait_recv()

    def own_sent():
        @pl.when(r == c)
        def _():
            for i in (2, 3):
                own_pack(i).wait_send()

        @pl.when(r > c)
        def _():
            for i in range(4):
                own_factor(i).wait_send()

    first = (r == 0) | (r == 2)

    @pl.when(((r == 1) | (r == 3)) & (r > c))
    def _():
        pl.semaphore_wait(gate, 1)

    @pl.when(r == c)
    def _():
        for i in (0, 1):
            own_pack(i).start()
        for i in (0, 1):
            own_pack(i).wait_send()
        for i in (2, 3):
            own_pack(i).start()

    @pl.when(first & (r == c))
    def _():
        pl.semaphore_signal(gate, inc=1, device_id=sibling, device_id_type=MESH)

    @pl.when(r > c)
    def _():
        own_factor(0).start()
        own_factor(1).start()

    for step, h in ((1, 0), (3, 1)):
        p, onward = pass_on(step, h)

        @pl.when(r == p)
        def _():
            pack_arrived(h)
            pass_pack(step, h).start()

        @pl.when(r > p)
        def _():
            factor_arrived(p, h)
            onward.start()

        @pl.when(r > c)
        def _():
            own_factor(2 + h).start()

    @pl.when(first & (r > c))
    def _():
        own_sent()
        pl.semaphore_signal(gate, inc=1, device_id=sibling, device_id_type=MESH)

    load_b.wait()

    def rest_of_factor(p):
        @pl.when(p == (c + 1) % PANELS)
        def _():
            factor_arrived(p, 0)

        @pl.when(p == (c + 3) % PANELS)
        def _():
            factor_arrived(p, 1)

        @pl.when(p == (c + 2) % PANELS)
        def _():
            factor_arrived(p, 0)
            factor_arrived(p, 1)

    def piece(p, q, s):
        return xbuf.at[p, s, pl.ds(q * QR, QR), :]

    def for_z(p, t, do):
        d = (z - p // 2 + NZ) % NZ
        mine = piece(p, 2 * t + k, y)
        far = d == 0
        near = (p < 2) & (y == 0)
        steps = (
            (4, 1, far & near),
            (0, 6, far & jnp.logical_not(near)),
            (1, -6, far),
            (2, 3, (far & jnp.logical_not(near)) | ((d == 3) & near)),
            (3, -3, far),
            (6, 2, (d == 6) | (d == 13) | ((d == 1) & near)),
            (7, -2, (d == 3) & jnp.logical_not(near)),
            (4, 1, ((d == 1) & near) | (d == 3) | (d == 6) | (d == 13) | (d == 10)),
            (5, -1, ((d == 3) & jnp.logical_not(near)) | (d == 6) | (d == 13) | (d == 10)),
        )
        for i, step, cond in steps:

            @pl.when(cond)
            def _():
                do(copy(mine, mine, zsend.at[p, t, i], zrecv.at[p, t], at_z(step)))

    def for_y(p, t, do):
        d = (z - p // 2 + NZ) % NZ
        mine = piece(p, 2 * t + k, y)
        for i in range(3):
            to = (y + i + 1) % NY

            @pl.when(((to != 0) & ((d != 0) | (y != 0) | (to != 2))) | ((to == 0) & (d != 0) & ((p >= 2) | (d != 1))))
            def _():
                do(copy(mine, mine, ysend.at[p, t, i], yrecv.at[p, t, y], dev(to, z, k)))

    def pass_first(p, t, do):
        @pl.when((z == p // 2) & (y == (1 if t == 0 else 3)))
        def _():
            it = piece(p, 2 * t + k, 0)
            do(copy(it, it, ysend.at[p, t, 3], yrecv.at[p, t, 0], dev(2, z, k)))

    def for_scatter(p, t, do):
        for s in (1, 3, 2):
            it = piece(p, 2 * t + k, s)
            do(copy(it, it, ssend.at[p, t, s], zrecv.at[p, t], dev(s, z, k)))

    def for_next(p, t, do):
        @pl.when(p < 2)
        def _():
            for s in range(1, NY):
                it = piece(p, 2 * t + k, s)
                do(copy(it, it, dsend.at[p, t, s], yrecv.at[p, t, s], at_z(1)))

    def to_sibling(p, q, s):
        it = piece(p, q, s)
        return copy(it, it, csend.at[p, q, s], crecv.at[p, q, s], sibling)

    def start(cp):
        cp.start()

    def wait_send(cp):
        cp.wait_send()

    def roles(p):
        chip = (y == 0) & (z == p // 2)
        source = r == p
        return source, chip & (r != p), jnp.logical_not(chip)

    def as_root(p, t, do):
        for_next(p, t, do)
        for_z(p, t, do)
        for_scatter(p, t, do)
        for_y(p, t, do)

    def prepare(p):
        rest_of_factor(p)
        high[...], low[...] = split(lbuf[p])

    def update(p):
        x = jnp.concatenate([xbuf[p, s] for s in range(NY)], axis=1)
        out[...] -= dot3((high[...], low[...]), split(x))

    def from_sibling(p):
        for t in range(2):
            for s in range(NY):
                to_sibling(p, 2 * t + 1 - k, s).wait_recv()

    def from_line(p):
        for t in range(2):
            for i in (1, 3, 2):
                s = (y + i) % NY
                it = piece(p, 2 * t + k, s)
                copy(it, it, ysend.at[p, t, 0], yrecv.at[p, t, s], sibling).wait_recv()

                @pl.when(s == 0)
                def _():
                    pass_first(p, t, start)

                to_sibling(p, 2 * t + k, s).start()

    def panel(p, carry):
        source, helper, other = roles(p)

        @pl.when(source)
        def _():
            @pl.when((p == (c + 1) % PANELS) | (p == (c + 2) % PANELS))
            def _():
                pack_arrived(0)

            @pl.when((p == (c + 3) % PANELS) | (p == (c + 2) % PANELS))
            def _():
                pack_arrived(1)

            for j, (r0, n) in enumerate(BLOCKS):
                solved = jnp.dot(pack[INV[j] : INV[j] + n, 0:n], out[r0 : r0 + n, :], precision=HI)
                out[r0 : r0 + n, :] = solved
                for s in range(NY):
                    xbuf[p, s, r0 : r0 + n, :] = solved[:, s * ST : (s + 1) * ST]
                for s in range(NY):
                    to_sibling(p, j, s).start()

                @pl.when((p % 2 == 1) & (k == j % 2))
                def _():
                    as_root(p, j // 2, start)

                if j < 3:
                    below = pack[BELOW[j] : BELOW[j] + PB - r0 - n, :]
                    out[r0 + n : PB, :] -= jnp.dot(below, solved, precision=HI)

            @pl.when(p % 2 == 0)
            def _():
                for t in range(2):
                    as_root(p, t, start)

        @pl.when(helper)
        def _():
            for t in range(2):
                for s in range(NY):
                    to_sibling(p, 2 * t + k, s).wait_recv()
                as_root(p, t, start)
            from_sibling(p)

        @pl.when(other)
        def _():
            for t in range(2):
                mine = piece(p, 2 * t + k, y)
                copy(mine, mine, zsend.at[p, t, 0], zrecv.at[p, t], sibling).wait_recv()
                for_z(p, t, start)
                for_y(p, t, start)
                to_sibling(p, 2 * t + k, y).start()

            @pl.when(r < PANELS)
            def _():
                from_line(p)
                from_sibling(p)

            @pl.when((r > PANELS - 1) & (p > 0))
            def _():
                from_line(p - 1)
                from_sibling(p - 1)
                prepare(p - 1)
                update(p - 1)

        @pl.when((r > p) & (r < PANELS))
        def _():
            prepare(p)
            update(p)

        return carry

    lax.fori_loop(0, PANELS, panel, 0)

    @pl.when(r > PANELS - 1)
    def _():
        prepare(PANELS - 1)
        from_line(PANELS - 1)
        from_sibling(PANELS - 1)
        update(PANELS - 1)

    def drain(p, carry):
        source, helper, other = roles(p)

        @pl.when(source)
        def _():
            for q in range(4):
                for s in range(NY):
                    to_sibling(p, q, s).wait_send()

        for t in range(2):

            @pl.when(source | helper)
            def _():
                for_next(p, t, wait_send)
                for_scatter(p, t, wait_send)

            for_z(p, t, wait_send)
            for_y(p, t, wait_send)

            @pl.when(other)
            def _():
                pass_first(p, t, wait_send)
                for s in range(NY):
                    to_sibling(p, 2 * t + k, s).wait_send()

        return carry

    lax.fori_loop(0, PANELS, drain, 0)

    @pl.when(jnp.logical_not(first & (r > c)))
    def _():
        own_sent()

    for step, h in ((1, 0), (3, 1)):
        p, onward = pass_on(step, h)

        @pl.when(r == p)
        def _():
            pass_pack(step, h).wait_send()

        @pl.when(r > p)
        def _():
            onward.wait_send()


def body(factor, slab):
    dma = pltpu.SemaphoreType.DMA
    return pl.pallas_call(
        kernel,
        out_shape=jax.ShapeDtypeStruct((PB, SLABC), jnp.float32),
        in_specs=[pl.BlockSpec(memory_space=pltpu.HBM)] * 2,
        out_specs=pl.BlockSpec(memory_space=pltpu.VMEM),
        scratch_shapes=[
            pltpu.VMEM((PANELS, PB, PB), jnp.float32),
            pltpu.VMEM((PB, PB), jnp.bfloat16),
            pltpu.VMEM((PB, PB), jnp.bfloat16),
            pltpu.VMEM((PACK, 128), jnp.float32),
            pltpu.VMEM((PANELS, NY, PB, ST), jnp.float32),
            dma((2,)),
            dma((6,)),
            dma((PANELS, 2)),
            dma((6,)),
            dma((2,)),
            dma((PANELS, 2, 8)),
            dma((PANELS, 2)),
            dma((PANELS, 2, 4)),
            dma((PANELS, 2, NY)),
            dma((PANELS, 4, NY)),
            dma((PANELS, 4, NY)),
            dma((PANELS, 2, NY)),
            dma((PANELS, 2, NY)),
            pltpu.SemaphoreType.REGULAR,
        ],
        compiler_params=pltpu.CompilerParams(
            collective_id=0, has_side_effects=True, vmem_limit_bytes=40 * 1024 * 1024
        ),
        cost_estimate=pl.CostEstimate(flops=2 * 3 * PB * 1664 * SLABC, bytes_accessed=2_500_000, transcendentals=0),
    )(factor, slab)


def solution(mesh):
    return jax.shard_map(
        body,
        mesh=mesh,
        in_specs=(P("rows", "cols"), P("rows", "cols")),
        out_specs=P("rows", "cols"),
        check_vma=False,
    )
```

```python
import functools

import jax
import jax.numpy as jnp
from jax import lax
from jax.experimental import pallas as pl
from jax.experimental.pallas import tpu as pltpu
from jax.sharding import PartitionSpec as P

MESH = pl.DeviceIdType.MESH
HI = lax.Precision.HIGHEST

PB = 416
PANELS = 4
SLABC = 512
HALF = PB // 2
QR = PB // 4
ST = 128
NY, NZ, NC = 4, 16, 2
BLOCKS = ((0, 128), (128, 128), (256, 128), (384, 32))
INV = (0, 416, 704, 864)
BELOW = (128, 544, 832)
PACK = 896
WAYS = ((1, 0), (3, 1), (1, 1), (3, 0))
PARTS = ((0, 416), (416, 480))


def split(value):
    high = value.astype(jnp.bfloat16)
    low = (value - high.astype(jnp.float32)).astype(jnp.bfloat16)
    return high, low


def dot3(left, right):
    dot = functools.partial(jnp.dot, preferred_element_type=jnp.float32)
    return dot(left[0], right[0]) + (dot(left[0], right[1]) + dot(left[1], right[0]))


def pack_panel(tri, pack):
    mats, outs = [], []
    for j, (r0, n) in enumerate(BLOCKS):
        if j < 3:
            pack[BELOW[j] : BELOW[j] + PB - r0 - n, :] = tri[r0 + n : PB, r0 : r0 + n]
        t = tri[r0 : r0 + n, r0 : r0 + n]
        row = lax.broadcasted_iota(jnp.int32, (n, n), 0)
        col = lax.broadcasted_iota(jnp.int32, (n, n), 1)
        mats.append((t, row, col))
        outs.append(jnp.where(row == col, 1.0 / jnp.where(row == col, t, 1.0), 0.0))
    m = 1
    while m < 128:
        for j, (r0, n) in enumerate(BLOCKS):
            if m >= n:
                continue
            t, row, col = mats[j]
            below = (row // (2 * m) == col // (2 * m)) & (row % (2 * m) >= m) & (col % (2 * m) < m)
            c = jnp.where(below, t, 0.0)
            o = outs[j]
            if m == 1:
                by_row = jnp.sum(o, axis=1, keepdims=True)
                by_col = jnp.sum(o, axis=0, keepdims=True)
                outs[j] = o - by_row * c * by_col
            else:
                outs[j] = o - jnp.dot(o, jnp.dot(c, o, precision=HI), precision=HI)
        m *= 2
    pack[INV[3] : PACK, :] = jnp.zeros((32, 128), jnp.float32)
    for j, (r0, n) in enumerate(BLOCKS):
        pack[INV[j] : INV[j] + n, 0:n] = outs[j]


def kernel(
    f_ref, b_ref, out, lbuf, high, low, pack, xbuf, load, lsend, lrecv, isend, irecv, zsend, zrecv, ysend, yrecv, csend, crecv, ssend, dsend, gate
):
    r = lax.axis_index("rows")
    c = lax.axis_index("cols")
    y = r // (NZ * NC)
    z = (r // NC) % NZ
    k = r % NC

    def dev(y_, z_, k_):
        return (y_ * (NZ * NC) + z_ * NC + k_, c)

    def at_x(step):
        return (r, (c + step) % PANELS)

    def at_y(step):
        return dev((y + step) % NY, z, k)

    def at_z(step):
        return dev(y, (z + step + NZ) % NZ, k)

    sibling = dev(y, z, 1 - k)

    barrier = pltpu.get_barrier_semaphore()
    partners = [at_x(1), at_x(2), at_x(3), at_y(1), at_y(2), at_y(3)]
    partners += [at_z(s) for s in (1, -1, 2, -2, 3, -3, 5, -5, 6, -6)] + [sibling]
    for partner in partners:
        pl.semaphore_signal(barrier, inc=1, device_id=partner, device_id_type=MESH)

    load_f = pltpu.make_async_copy(f_ref, lbuf.at[c], load.at[0])
    load_b = pltpu.make_async_copy(b_ref, out, load.at[1])
    load_f.start()
    load_b.start()
    load_f.wait()

    @pl.when(r == c)
    def _():
        pack_panel(lbuf.at[c], pack)

    pl.semaphore_wait(barrier, len(partners))

    def copy(src, dst, send, recv, to):
        return pltpu.make_async_remote_copy(
            src_ref=src, dst_ref=dst, send_sem=send, recv_sem=recv, device_id=to, device_id_type=MESH
        )

    def lhalf(p, h):
        return lbuf.at[p, pl.ds(h * HALF, HALF), :]

    def ppart(h):
        return pack.at[pl.ds(PARTS[h][0], PARTS[h][1]), :]

    def own_pack(i):
        step, h = WAYS[i]
        return copy(ppart(h), ppart(h), isend.at[i], irecv.at[h], at_x(step))

    def pass_pack(step, h):
        return copy(ppart(h), ppart(h), isend.at[4 + h], irecv.at[h], at_x(step))

    def pack_arrived(h):
        copy(ppart(h), ppart(h), isend.at[0], irecv.at[h], sibling).wait_recv()

    def own_factor(i):
        step, h = WAYS[i]
        return copy(lhalf(c, h), lhalf(c, h), lsend.at[i], lrecv.at[c, h], at_x(step))

    def pass_on(step, h):
        p = (c + 4 - step) % PANELS
        return p, copy(lhalf(p, h), lhalf(p, h), lsend.at[4 + h], lrecv.at[p, h], at_x(step))

    def factor_arrived(p, h):
        copy(lhalf(p, h), lhalf(p, h), lsend.at[0], lrecv.at[p, h], sibling).wait_recv()

    def own_sent():
        @pl.when(r == c)
        def _():
            for i in (2, 3):
                own_pack(i).wait_send()

        @pl.when((r > c) & jnp.logical_not(first))
        def _():
            for i in (0, 1):
                own_factor(i).wait_send()

        @pl.when(r > c)
        def _():
            for i in (2, 3):
                own_factor(i).wait_send()

    first = (r == 0) | (r == 2)

    @pl.when(((r == 1) | (r == 3)) & (r > c))
    def _():
        pl.semaphore_wait(gate, 1)

    @pl.when(r == c)
    def _():
        for i in (0, 1):
            own_pack(i).start()
        for i in (0, 1):
            own_pack(i).wait_send()
        for i in (2, 3):
            own_pack(i).start()

    @pl.when(first & (r == c))
    def _():
        pl.semaphore_signal(gate, inc=1, device_id=sibling, device_id_type=MESH)

    @pl.when(r > c)
    def _():
        own_factor(0).start()
        own_factor(1).start()

    @pl.when(first & (r > c))
    def _():
        own_factor(0).wait_send()
        own_factor(1).wait_send()
        pl.semaphore_signal(gate, inc=1, device_id=sibling, device_id_type=MESH)

    for step, h in ((1, 0), (3, 1)):
        p, onward = pass_on(step, h)

        @pl.when(r == p)
        def _():
            pack_arrived(h)
            pass_pack(step, h).start()

        @pl.when(r > p)
        def _():
            factor_arrived(p, h)
            onward.start()

        @pl.when(r > c)
        def _():
            own_factor(2 + h).start()

    load_b.wait()

    def rest_of_factor(p):
        @pl.when(p == (c + 1) % PANELS)
        def _():
            factor_arrived(p, 0)

        @pl.when(p == (c + 3) % PANELS)
        def _():
            factor_arrived(p, 1)

        @pl.when(p == (c + 2) % PANELS)
        def _():
            factor_arrived(p, 0)
            factor_arrived(p, 1)

    def piece(p, q, s):
        return xbuf.at[p, s, pl.ds(q * QR, QR), :]

    def for_z(p, t, do):
        d = (z - p // 2 + NZ) % NZ
        mine = piece(p, 2 * t + k, y)
        far = d == 0
        near = (p < 2) & (y == 0)
        steps = (
            (4, 1, far & near),
            (0, 6, far & jnp.logical_not(near)),
            (1, -5, far),
            (2, 3, (far & jnp.logical_not(near)) | ((d == 3) & near)),
            (3, -2, far | (d == 11)),
            (6, 2, (d == 6) | ((d == 1) & near)),
            (7, -2, (d == 3) & jnp.logical_not(near)),
            (4, 1, ((d == 1) & near) | (d == 3) | (d == 6) | (d == 14) | (d == 11)),
            (5, -1, ((d == 3) & jnp.logical_not(near)) | (d == 6) | (d == 14) | (d == 11)),
        )
        for i, step, cond in steps:

            @pl.when(cond)
            def _():
                do(copy(mine, mine, zsend.at[p, t, i], zrecv.at[p, t], at_z(step)))

    def for_y(p, t, do):
        d = (z - p // 2 + NZ) % NZ
        mine = piece(p, 2 * t + k, y)
        for i in range(3):
            to = (y + i + 1) % NY

            @pl.when(((to != 0) & ((d != 0) | (y != 0) | (to != 2))) | ((to == 0) & (d != 0) & ((p >= 2) | (d != 1))))
            def _():
                do(copy(mine, mine, ysend.at[p, t, i], yrecv.at[p, t, y], dev(to, z, k)))

    def pass_first(p, t, do):
        @pl.when((z == p // 2) & (y == (1 if t == 0 else 3)))
        def _():
            it = piece(p, 2 * t + k, 0)
            do(copy(it, it, ysend.at[p, t, 3], yrecv.at[p, t, 0], dev(2, z, k)))

    def for_scatter(p, t, do):
        for s in (1, 3, 2):
            it = piece(p, 2 * t + k, s)
            do(copy(it, it, ssend.at[p, t, s], zrecv.at[p, t], dev(s, z, k)))

    def for_next(p, t, do):
        @pl.when(p < 2)
        def _():
            for s in range(1, NY):
                it = piece(p, 2 * t + k, s)
                do(copy(it, it, dsend.at[p, t, s], yrecv.at[p, t, s], at_z(1)))

    def to_sibling(p, q, s):
        it = piece(p, q, s)
        return copy(it, it, csend.at[p, q, s], crecv.at[p, q, s], sibling)

    def start(cp):
        cp.start()

    def wait_send(cp):
        cp.wait_send()

    def roles(p):
        chip = (y == 0) & (z == p // 2)
        source = r == p
        return source, chip & (r != p), jnp.logical_not(chip)

    def as_root(p, t, do):
        for_next(p, t, do)
        for_z(p, t, do)
        for_scatter(p, t, do)
        for_y(p, t, do)

    def prepare(p):
        rest_of_factor(p)
        high[...], low[...] = split(lbuf[p])

    def update(p):
        x = jnp.concatenate([xbuf[p, s] for s in range(NY)], axis=1)
        out[...] -= dot3((high[...], low[...]), split(x))

    def from_sibling(p):
        for t in range(2):
            for s in range(NY):
                to_sibling(p, 2 * t + 1 - k, s).wait_recv()

    def from_line(p):
        for t in range(2):
            for i in (1, 3, 2):
                s = (y + i) % NY
                it = piece(p, 2 * t + k, s)
                copy(it, it, ysend.at[p, t, 0], yrecv.at[p, t, s], sibling).wait_recv()

                @pl.when(s == 0)
                def _():
                    pass_first(p, t, start)

                to_sibling(p, 2 * t + k, s).start()

    def panel(p, carry):
        source, helper, other = roles(p)

        @pl.when(source)
        def _():
            @pl.when((p == (c + 1) % PANELS) | (p == (c + 2) % PANELS))
            def _():
                pack_arrived(0)

            @pl.when((p == (c + 3) % PANELS) | (p == (c + 2) % PANELS))
            def _():
                pack_arrived(1)

            for j, (r0, n) in enumerate(BLOCKS):
                solved = jnp.dot(pack[INV[j] : INV[j] + n, 0:n], out[r0 : r0 + n, :], precision=HI)
                out[r0 : r0 + n, :] = solved
                for s in range(NY):
                    xbuf[p, s, r0 : r0 + n, :] = solved[:, s * ST : (s + 1) * ST]
                for s in range(NY):
                    to_sibling(p, j, s).start()

                @pl.when((p % 2 == 1) & (k == j % 2))
                def _():
                    as_root(p, j // 2, start)

                if j < 3:
                    below = pack[BELOW[j] : BELOW[j] + PB - r0 - n, :]
                    out[r0 + n : PB, :] -= jnp.dot(below, solved, precision=HI)

            @pl.when(p % 2 == 0)
            def _():
                for t in range(2):
                    as_root(p, t, start)

        @pl.when(helper)
        def _():
            for t in range(2):
                for s in range(NY):
                    to_sibling(p, 2 * t + k, s).wait_recv()
                as_root(p, t, start)
            from_sibling(p)

        @pl.when(other)
        def _():
            for t in range(2):
                mine = piece(p, 2 * t + k, y)
                copy(mine, mine, zsend.at[p, t, 0], zrecv.at[p, t], sibling).wait_recv()
                for_z(p, t, start)
                for_y(p, t, start)
                to_sibling(p, 2 * t + k, y).start()

            @pl.when(r < PANELS)
            def _():
                from_line(p)
                from_sibling(p)

            @pl.when((r > PANELS - 1) & (p > 0))
            def _():
                from_line(p - 1)
                from_sibling(p - 1)
                prepare(p - 1)
                update(p - 1)

        @pl.when((r > p) & (r < PANELS))
        def _():
            prepare(p)
            update(p)

        return carry

    lax.fori_loop(0, PANELS, panel, 0)

    @pl.when(r > PANELS - 1)
    def _():
        prepare(PANELS - 1)
        from_line(PANELS - 1)
        from_sibling(PANELS - 1)
        update(PANELS - 1)

    def drain(p, carry):
        source, helper, other = roles(p)

        @pl.when(source)
        def _():
            for q in range(4):
                for s in range(NY):
                    to_sibling(p, q, s).wait_send()

        for t in range(2):

            @pl.when(source | helper)
            def _():
                for_next(p, t, wait_send)
                for_scatter(p, t, wait_send)

            for_z(p, t, wait_send)
            for_y(p, t, wait_send)

            @pl.when(other)
            def _():
                pass_first(p, t, wait_send)
                for s in range(NY):
                    to_sibling(p, 2 * t + k, s).wait_send()

        return carry

    lax.fori_loop(0, PANELS, drain, 0)

    own_sent()

    for step, h in ((1, 0), (3, 1)):
        p, onward = pass_on(step, h)

        @pl.when(r == p)
        def _():
            pass_pack(step, h).wait_send()

        @pl.when(r > p)
        def _():
            onward.wait_send()


def body(factor, slab):
    dma = pltpu.SemaphoreType.DMA
    return pl.pallas_call(
        kernel,
        out_shape=jax.ShapeDtypeStruct((PB, SLABC), jnp.float32),
        in_specs=[pl.BlockSpec(memory_space=pltpu.HBM)] * 2,
        out_specs=pl.BlockSpec(memory_space=pltpu.VMEM),
        scratch_shapes=[
            pltpu.VMEM((PANELS, PB, PB), jnp.float32),
            pltpu.VMEM((PB, PB), jnp.bfloat16),
            pltpu.VMEM((PB, PB), jnp.bfloat16),
            pltpu.VMEM((PACK, 128), jnp.float32),
            pltpu.VMEM((PANELS, NY, PB, ST), jnp.float32),
            dma((2,)),
            dma((6,)),
            dma((PANELS, 2)),
            dma((6,)),
            dma((2,)),
            dma((PANELS, 2, 8)),
            dma((PANELS, 2)),
            dma((PANELS, 2, 4)),
            dma((PANELS, 2, NY)),
            dma((PANELS, 4, NY)),
            dma((PANELS, 4, NY)),
            dma((PANELS, 2, NY)),
            dma((PANELS, 2, NY)),
            pltpu.SemaphoreType.REGULAR,
        ],
        compiler_params=pltpu.CompilerParams(
            collective_id=0, has_side_effects=True, vmem_limit_bytes=40 * 1024 * 1024
        ),
        cost_estimate=pl.CostEstimate(flops=2 * 3 * PB * 1664 * SLABC, bytes_accessed=2_500_000, transcendentals=0),
    )(factor, slab)


def solution(mesh):
    return jax.shard_map(
        body,
        mesh=mesh,
        in_specs=(P("rows", "cols"), P("rows", "cols")),
        out_specs=P("rows", "cols"),
        check_vma=False,
    )
```

```python
import functools

import jax
import jax.numpy as jnp
from jax import lax
from jax.experimental import pallas as pl
from jax.experimental.pallas import tpu as pltpu
from jax.sharding import PartitionSpec as P

MESH = pl.DeviceIdType.MESH
HI = lax.Precision.HIGHEST

PB = 416
PANELS = 4
SLABC = 512
HALF = PB // 2
QR = PB // 4
ST = 128
NY, NZ, NC = 4, 16, 2
BLOCKS = ((0, 128), (128, 128), (256, 128), (384, 32))
INV = (0, 416, 704, 864)
BELOW = (128, 544, 832)
PACK = 896
WAYS = ((1, 0), (3, 1), (1, 1), (3, 0))
PARTS = ((0, 416), (416, 480))


def split(value):
    high = value.astype(jnp.bfloat16)
    low = (value - high.astype(jnp.float32)).astype(jnp.bfloat16)
    return high, low


def dot3(left, right):
    dot = functools.partial(jnp.dot, preferred_element_type=jnp.float32)
    return dot(left[0], right[0]) + (dot(left[0], right[1]) + dot(left[1], right[0]))


def pack_panel(tri, pack):
    mats, outs = [], []
    for j, (r0, n) in enumerate(BLOCKS):
        if j < 3:
            pack[BELOW[j] : BELOW[j] + PB - r0 - n, :] = tri[r0 + n : PB, r0 : r0 + n]
        t = tri[r0 : r0 + n, r0 : r0 + n]
        row = lax.broadcasted_iota(jnp.int32, (n, n), 0)
        col = lax.broadcasted_iota(jnp.int32, (n, n), 1)
        mats.append((t, row, col))
        outs.append(jnp.where(row == col, 1.0 / jnp.where(row == col, t, 1.0), 0.0))
    m = 1
    while m < 128:
        for j, (r0, n) in enumerate(BLOCKS):
            if m >= n:
                continue
            t, row, col = mats[j]
            below = (row // (2 * m) == col // (2 * m)) & (row % (2 * m) >= m) & (col % (2 * m) < m)
            c = jnp.where(below, t, 0.0)
            o = outs[j]
            if m == 1:
                by_row = jnp.sum(o, axis=1, keepdims=True)
                by_col = jnp.sum(o, axis=0, keepdims=True)
                outs[j] = o - by_row * c * by_col
            else:
                outs[j] = o - jnp.dot(o, jnp.dot(c, o, precision=HI), precision=HI)
        m *= 2
    pack[INV[3] : PACK, :] = jnp.zeros((32, 128), jnp.float32)
    for j, (r0, n) in enumerate(BLOCKS):
        pack[INV[j] : INV[j] + n, 0:n] = outs[j]


def kernel(
    f_ref, b_ref, out, lbuf, high, low, pack, xbuf, load, lsend, lrecv, isend, irecv, zsend, zrecv, ysend, yrecv, csend, crecv, ssend, dsend, gate
):
    r = lax.axis_index("rows")
    c = lax.axis_index("cols")
    y = r // (NZ * NC)
    z = (r // NC) % NZ
    k = r % NC

    def dev(y_, z_, k_):
        return (y_ * (NZ * NC) + z_ * NC + k_, c)

    def at_x(step):
        return (r, (c + step) % PANELS)

    def at_y(step):
        return dev((y + step) % NY, z, k)

    def at_z(step):
        return dev(y, (z + step + NZ) % NZ, k)

    sibling = dev(y, z, 1 - k)

    barrier = pltpu.get_barrier_semaphore()
    partners = [at_x(1), at_x(2), at_x(3), at_y(1), at_y(2), at_y(3)]
    partners += [at_z(s) for s in (1, -1, 2, -2, 3, -3, 5, -5, 6, -6)] + [sibling]
    for partner in partners:
        pl.semaphore_signal(barrier, inc=1, device_id=partner, device_id_type=MESH)

    load_f = pltpu.make_async_copy(f_ref, lbuf.at[c], load.at[0])
    load_b = pltpu.make_async_copy(b_ref, out, load.at[1])
    load_f.start()
    load_b.start()
    load_f.wait()

    @pl.when(r == c)
    def _():
        pack_panel(lbuf.at[c], pack)

    pl.semaphore_wait(barrier, len(partners))

    def copy(src, dst, send, recv, to):
        return pltpu.make_async_remote_copy(
            src_ref=src, dst_ref=dst, send_sem=send, recv_sem=recv, device_id=to, device_id_type=MESH
        )

    def lhalf(p, h):
        return lbuf.at[p, pl.ds(h * HALF, HALF), :]

    def ppart(h):
        return pack.at[pl.ds(PARTS[h][0], PARTS[h][1]), :]

    def own_pack(i):
        step, h = WAYS[i]
        return copy(ppart(h), ppart(h), isend.at[i], irecv.at[h], at_x(step))

    def pass_pack(step, h):
        return copy(ppart(h), ppart(h), isend.at[4 + h], irecv.at[h], at_x(step))

    def pack_arrived(h):
        copy(ppart(h), ppart(h), isend.at[0], irecv.at[h], sibling).wait_recv()

    def own_factor(i):
        step, h = WAYS[i]
        return copy(lhalf(c, h), lhalf(c, h), lsend.at[i], lrecv.at[c, h], at_x(step))

    def pass_on(step, h):
        p = (c + 4 - step) % PANELS
        return p, copy(lhalf(p, h), lhalf(p, h), lsend.at[4 + h], lrecv.at[p, h], at_x(step))

    def factor_arrived(p, h):
        copy(lhalf(p, h), lhalf(p, h), lsend.at[0], lrecv.at[p, h], sibling).wait_recv()

    def own_sent():
        @pl.when(r == c)
        def _():
            for i in (2, 3):
                own_pack(i).wait_send()

        @pl.when((r > c) & jnp.logical_not(first))
        def _():
            for i in (0, 1):
                own_factor(i).wait_send()

        @pl.when(r > c)
        def _():
            for i in (2, 3):
                own_factor(i).wait_send()

    first = (r == 0) | (r == 2)

    @pl.when((r == 1) & (r - 1 >= c))
    def _():
        pl.semaphore_wait(gate, 1)

    @pl.when(r == c)
    def _():
        for i in (0, 1):
            own_pack(i).start()
        for i in (0, 1):
            own_pack(i).wait_send()
        for i in (2, 3):
            own_pack(i).start()

    @pl.when((r == 0) & (c == 0))
    def _():
        pl.semaphore_signal(gate, inc=1, device_id=sibling, device_id_type=MESH)

    @pl.when(r > c)
    def _():
        own_factor(0).start()
        own_factor(1).start()

    @pl.when(first & (r > c))
    def _():
        own_factor(0).wait_send()
        own_factor(1).wait_send()

    for step, h in ((1, 0), (3, 1)):
        p, onward = pass_on(step, h)

        @pl.when(r == p)
        def _():
            pack_arrived(h)
            pass_pack(step, h).start()

        @pl.when(r > p)
        def _():
            factor_arrived(p, h)
            onward.start()

        @pl.when(r > c)
        def _():
            own_factor(2 + h).start()

    load_b.wait()

    def rest_of_factor(p):
        @pl.when(p == (c + 1) % PANELS)
        def _():
            factor_arrived(p, 0)

        @pl.when(p == (c + 3) % PANELS)
        def _():
            factor_arrived(p, 1)

        @pl.when(p == (c + 2) % PANELS)
        def _():
            factor_arrived(p, 0)
            factor_arrived(p, 1)

    def piece(p, q, s):
        return xbuf.at[p, s, pl.ds(q * QR, QR), :]

    def for_z(p, t, do):
        d = (z - p // 2 + NZ) % NZ
        mine = piece(p, 2 * t + k, y)
        far = d == 0
        near = (p < 2) & (y == 0)
        steps = (
            (4, 1, far & near),
            (0, 6, far & jnp.logical_not(near)),
            (1, -5, far),
            (2, 3, (far & jnp.logical_not(near)) | ((d == 3) & near)),
            (3, -2, far | (d == 11)),
            (6, 2, (d == 6) | ((d == 1) & near)),
            (7, -2, (d == 3) & jnp.logical_not(near)),
            (4, 1, ((d == 1) & near) | (d == 3) | (d == 6) | (d == 14) | (d == 11)),
            (5, -1, ((d == 3) & jnp.logical_not(near)) | (d == 6) | (d == 14) | (d == 11)),
        )
        for i, step, cond in steps:

            @pl.when(cond)
            def _():
                do(copy(mine, mine, zsend.at[p, t, i], zrecv.at[p, t], at_z(step)))

    def for_y(p, t, do):
        d = (z - p // 2 + NZ) % NZ
        mine = piece(p, 2 * t + k, y)
        for i in range(3):
            to = (y + i + 1) % NY

            @pl.when(((to != 0) & ((d != 0) | (y != 0) | (to != 2))) | ((to == 0) & (d != 0) & ((p >= 2) | (d != 1))))
            def _():
                do(copy(mine, mine, ysend.at[p, t, i], yrecv.at[p, t, y], dev(to, z, k)))

    def pass_first(p, t, do):
        @pl.when((z == p // 2) & (y == (1 if t == 0 else 3)))
        def _():
            it = piece(p, 2 * t + k, 0)
            do(copy(it, it, ysend.at[p, t, 3], yrecv.at[p, t, 0], dev(2, z, k)))

    def for_scatter(p, t, do):
        for s in (1, 3, 2):
            it = piece(p, 2 * t + k, s)
            do(copy(it, it, ssend.at[p, t, s], zrecv.at[p, t], dev(s, z, k)))

    def for_next(p, t, do):
        @pl.when(p < 2)
        def _():
            for s in range(1, NY):
                it = piece(p, 2 * t + k, s)
                do(copy(it, it, dsend.at[p, t, s], yrecv.at[p, t, s], at_z(1)))

    def to_sibling(p, q, s):
        it = piece(p, q, s)
        return copy(it, it, csend.at[p, q, s], crecv.at[p, q, s], sibling)

    def start(cp):
        cp.start()

    def wait_send(cp):
        cp.wait_send()

    def roles(p):
        chip = (y == 0) & (z == p // 2)
        source = r == p
        return source, chip & (r != p), jnp.logical_not(chip)

    def as_root(p, t, do):
        for_next(p, t, do)
        for_z(p, t, do)
        for_scatter(p, t, do)
        for_y(p, t, do)

    def prepare(p):
        rest_of_factor(p)
        high[...], low[...] = split(lbuf[p])

    def update(p):
        x = jnp.concatenate([xbuf[p, s] for s in range(NY)], axis=1)
        out[...] -= dot3((high[...], low[...]), split(x))

    def from_sibling(p):
        for t in range(2):
            for s in range(NY):
                to_sibling(p, 2 * t + 1 - k, s).wait_recv()

    def from_line(p):
        for t in range(2):
            for i in (1, 3, 2):
                s = (y + i) % NY
                it = piece(p, 2 * t + k, s)
                copy(it, it, ysend.at[p, t, 0], yrecv.at[p, t, s], sibling).wait_recv()

                @pl.when(s == 0)
                def _():
                    pass_first(p, t, start)

                to_sibling(p, 2 * t + k, s).start()

    def panel(p, carry):
        source, helper, other = roles(p)

        @pl.when(source)
        def _():
            @pl.when((p == (c + 1) % PANELS) | (p == (c + 2) % PANELS))
            def _():
                pack_arrived(0)

            @pl.when((p == (c + 3) % PANELS) | (p == (c + 2) % PANELS))
            def _():
                pack_arrived(1)

            for j, (r0, n) in enumerate(BLOCKS):
                solved = jnp.dot(pack[INV[j] : INV[j] + n, 0:n], out[r0 : r0 + n, :], precision=HI)
                out[r0 : r0 + n, :] = solved
                for s in range(NY):
                    xbuf[p, s, r0 : r0 + n, :] = solved[:, s * ST : (s + 1) * ST]
                for s in range(NY):
                    to_sibling(p, j, s).start()

                @pl.when((p % 2 == 1) & (k == j % 2))
                def _():
                    as_root(p, j // 2, start)

                if j < 3:
                    below = pack[BELOW[j] : BELOW[j] + PB - r0 - n, :]
                    out[r0 + n : PB, :] -= jnp.dot(below, solved, precision=HI)

            @pl.when(p % 2 == 0)
            def _():
                for t in range(2):
                    as_root(p, t, start)

        @pl.when(helper)
        def _():
            for t in range(2):
                for s in range(NY):
                    to_sibling(p, 2 * t + k, s).wait_recv()
                as_root(p, t, start)
            from_sibling(p)

        @pl.when(other)
        def _():
            for t in range(2):
                mine = piece(p, 2 * t + k, y)
                copy(mine, mine, zsend.at[p, t, 0], zrecv.at[p, t], sibling).wait_recv()
                for_z(p, t, start)
                for_y(p, t, start)
                to_sibling(p, 2 * t + k, y).start()

            @pl.when(r < PANELS)
            def _():
                from_line(p)
                from_sibling(p)

            @pl.when((r > PANELS - 1) & (p > 0))
            def _():
                from_line(p - 1)
                from_sibling(p - 1)
                prepare(p - 1)
                update(p - 1)

        @pl.when((r > p) & (r < PANELS))
        def _():
            prepare(p)
            update(p)

        return carry

    lax.fori_loop(0, PANELS, panel, 0)

    @pl.when(r > PANELS - 1)
    def _():
        prepare(PANELS - 1)
        from_line(PANELS - 1)
        from_sibling(PANELS - 1)
        update(PANELS - 1)

    def drain(p, carry):
        source, helper, other = roles(p)

        @pl.when(source)
        def _():
            for q in range(4):
                for s in range(NY):
                    to_sibling(p, q, s).wait_send()

        for t in range(2):

            @pl.when(source | helper)
            def _():
                for_next(p, t, wait_send)
                for_scatter(p, t, wait_send)

            for_z(p, t, wait_send)
            for_y(p, t, wait_send)

            @pl.when(other)
            def _():
                pass_first(p, t, wait_send)
                for s in range(NY):
                    to_sibling(p, 2 * t + k, s).wait_send()

        return carry

    lax.fori_loop(0, PANELS, drain, 0)

    own_sent()

    for step, h in ((1, 0), (3, 1)):
        p, onward = pass_on(step, h)

        @pl.when(r == p)
        def _():
            pass_pack(step, h).wait_send()

        @pl.when(r > p)
        def _():
            onward.wait_send()


def body(factor, slab):
    dma = pltpu.SemaphoreType.DMA
    return pl.pallas_call(
        kernel,
        out_shape=jax.ShapeDtypeStruct((PB, SLABC), jnp.float32),
        in_specs=[pl.BlockSpec(memory_space=pltpu.HBM)] * 2,
        out_specs=pl.BlockSpec(memory_space=pltpu.VMEM),
        scratch_shapes=[
            pltpu.VMEM((PANELS, PB, PB), jnp.float32),
            pltpu.VMEM((PB, PB), jnp.bfloat16),
            pltpu.VMEM((PB, PB), jnp.bfloat16),
            pltpu.VMEM((PACK, 128), jnp.float32),
            pltpu.VMEM((PANELS, NY, PB, ST), jnp.float32),
            dma((2,)),
            dma((6,)),
            dma((PANELS, 2)),
            dma((6,)),
            dma((2,)),
            dma((PANELS, 2, 8)),
            dma((PANELS, 2)),
            dma((PANELS, 2, 4)),
            dma((PANELS, 2, NY)),
            dma((PANELS, 4, NY)),
            dma((PANELS, 4, NY)),
            dma((PANELS, 2, NY)),
            dma((PANELS, 2, NY)),
            pltpu.SemaphoreType.REGULAR,
        ],
        compiler_params=pltpu.CompilerParams(
            collective_id=0, has_side_effects=True, vmem_limit_bytes=40 * 1024 * 1024
        ),
        cost_estimate=pl.CostEstimate(flops=2 * 3 * PB * 1664 * SLABC, bytes_accessed=2_500_000, transcendentals=0),
    )(factor, slab)


def solution(mesh):
    return jax.shard_map(
        body,
        mesh=mesh,
        in_specs=(P("rows", "cols"), P("rows", "cols")),
        out_specs=P("rows", "cols"),
        check_vma=False,
    )
```
